256 devices in a mesh: dir: 4 (over x_lo, core), bond: 64 (over y, z, x_hi).
Axes of the slice: x: 4 (x_hi: 2, x_lo: 2; x = x_hi * 2 + x_lo), y: 4, z: 8, core: 2. Of those that a mesh axis runs over, the one named last changes fastest.
Arguments:
- corner_mat: bfloat16 [4, 8192, 8192], P('dir', 'bond'), may hold values from -0.0625 to 0.0625
- edge_mat: bfloat16 [4, 32768, 8192], P('dir', 'bond'), may hold values from -0.0625 to 0.0625
- edge_panel: bfloat16 [4, 8192, 512], P('dir', 'bond'), may hold values from -6 to 6
- vertex_weights: float32 [4, 4, 4], replicated, may hold values from -3 to 3
- projector: bfloat16 [4, 512, 256], P('dir'), may hold values from -0.25 to 0.25
- edge_projector: bfloat16 [4, 8192, 256], P('dir', 'bond'), may hold values from -0.1875 to 0.1875
Outputs:
- new_corner: bfloat16 [4, 32768, 256], P('dir', 'bond')
- gram: float32 [4, 256, 256], P('dir', 'bond')
- new_edge: bfloat16 [4, 256, 512], P('dir', 'bond')
The draws below stay inside these ranges and needn't reach their ends.
All inputs are finite; a program needn't handle non-finite values.
Results may differ from the reference program's by a relative error of at most 0.0065.
Values may be sent and summed in bfloat16 or wider, within the bound.
No kernel may reach another device: no remote copies, remote signals or barrier semaphores. Data moves between devices by JAX's collectives and lax.ppermute only.
A program may use at most 128 MiB of HBM per device.

```python
import jax
import jax.numpy as jnp
from jax import lax

CHI = 8192
D = 4
PANEL = 512
KEEP = 256


def with_spikes(array, key, source, target, blocks, factor):
    owner, partner = [(jnp.arange(array.shape[axis_at]) // (array.shape[axis_at] // blocks)).reshape([-1 if axis == axis_at else 1 for axis in range(array.ndim)]) for axis_at in (source, target)]
    chosen = jax.random.permutation(key, blocks)[partner]
    strong = (owner == chosen) | (owner == (partner + blocks // 2) % blocks)
    return jnp.where(strong, factor * array, array)


def steps_of(key, dims, cuts, least, top_value):
    def one(axis_at, shards_of):
        heights = jax.random.uniform(jax.random.fold_in(jax.random.fold_in(key, 6), axis_at), (shards_of,), jnp.float32, least / len(cuts), top_value / len(cuts))
        return jnp.repeat(jnp.exp(heights), dims[axis_at] // shards_of).reshape((-1,) + (1,) * (len(dims) - axis_at - 1))

    level = one(*cuts[0])
    for cut in cuts[1:]:
        level = level * one(*cut)
    return level


def bell_draw(key, shape, scale, reach, cuts=(), held_as=jnp.bfloat16):
    values = jax.random.normal(key, shape, jnp.float32) * scale
    if len(cuts) > 0:
        values = steps_of(key, shape, cuts, -0.22, 0.18) * values
    return jnp.clip(values, min=-reach, max=reach).astype(held_as)


def bell_draw_with(key, extent, scale, most, split, heavy, held_as=jnp.bfloat16):
    result = scale * jax.random.normal(key, extent, jnp.float32)
    if split:
        result = result * steps_of(key, extent, split, -0.22, 0.18)
    return jnp.clip(with_spikes(result, jax.random.fold_in(key, 3), *heavy), -most, most).astype(held_as)


def setup_inputs(seed: int = 0) -> dict:
    seeds = jax.random.split(jax.random.key(seed), 7)
    return {
        "corner_mat": bell_draw(seeds[0], (4, CHI, CHI), CHI ** -0.5, 0.0625, ((0, 4), (1, 64))),
        "edge_mat": bell_draw(seeds[1], (4, CHI * D, CHI), CHI ** -0.5, 0.0625, ((0, 4), (1, 64))),
        "edge_panel": bell_draw(seeds[2], (4, CHI, PANEL), 1.0, 6.0, ((0, 4), (1, 64))),
        "vertex_weights": bell_draw(seeds[3], (D, D, D), D ** -0.5, 3.0, (), jnp.float32),
        "projector": bell_draw(seeds[4], (4, PANEL, KEEP), PANEL ** -0.5, 0.25, ((0, 4),)),
        "edge_projector": bell_draw_with(seeds[5], (4, CHI, KEEP), CHI ** -0.5, 0.1875, ((0, 4), (1, 64)), (1, 2, 64, 4.0)),
    }


def enlarge(previous, hidden_panel, vertex_weights):
    raw_block = jnp.dot(previous, hidden_panel, preferred_element_type=jnp.float32)
    row_count = raw_block.shape[0] // D
    split_block = raw_block.reshape(row_count, D, D, PANEL // D)
    mixed_block = jnp.einsum("isub,sut->istb", split_block, vertex_weights, precision=lax.Precision.HIGHEST)
    return mixed_block.reshape(row_count * D, PANEL).astype(jnp.bfloat16)


def reference(corner_mat, edge_mat, edge_panel, vertex_weights, projector, edge_projector):
    corners_out = []
    grams_out = []
    edges_out = []
    for direction in range(4):
        hidden_panel = jnp.dot(corner_mat[direction], edge_panel[direction], preferred_element_type=jnp.float32).astype(jnp.bfloat16)
        enlarged = enlarge(edge_mat[(direction - 1) % 4], hidden_panel, vertex_weights)
        projected = jnp.dot(enlarged, projector[direction], preferred_element_type=jnp.float32)
        corners_out.append(projected.astype(jnp.bfloat16))
        grams_out.append(jnp.dot(projected.T, projected, precision=lax.Precision.HIGHEST) / (CHI * D))
        edges_out.append(jnp.dot(edge_projector[direction].T, edge_panel[direction], preferred_element_type=jnp.float32).astype(jnp.bfloat16))
    return jnp.stack(corners_out), jnp.stack(grams_out), jnp.stack(edges_out)
```

```python
import jax
import jax.numpy as jnp
from jax import lax
from jax.sharding import PartitionSpec as P

CHI = 8192
D = 4
PANEL = 512
KEEP = 256


def passed_along(block, axis, distance):
    devices = range(lax.axis_size(axis))
    route = [((i - distance) % len(devices), i) for i in devices]
    return lax.ppermute(block, axis, route)


def enlarge(raw_block, vertex_weights):
    row_count = raw_block.shape[0] // D
    split_block = raw_block.reshape(row_count, D, D, PANEL // D)
    mixed_block = jnp.einsum(
        "isub,sut->istb", split_block, vertex_weights, precision=lax.Precision.HIGHEST
    )
    return mixed_block.reshape(row_count * D, PANEL).astype(jnp.bfloat16)


def on_device(corner_mat, edge_mat, edge_panel, vertex_weights, projector, edge_projector):
    corner_rows = corner_mat[0]
    own_edge = edge_mat[0]
    panel_rows = edge_panel[0]
    proj_next = passed_along(projector[0], "dir", -1)
    edge_proj_rows = lax.all_to_all(
        edge_projector[0].T, "bond", split_axis=0, concat_axis=1, tiled=True
    )
    panel_full = lax.all_gather(panel_rows, "bond", axis=0, tiled=True)
    hidden_panel = jnp.dot(
        corner_rows, panel_full, preferred_element_type=jnp.float32
    ).astype(jnp.bfloat16)
    hidden_full = lax.all_gather(
        passed_along(hidden_panel, "dir", -1), "bond", axis=0, tiled=True
    )
    new_edge = jnp.dot(
        edge_proj_rows, panel_full, preferred_element_type=jnp.float32
    ).astype(jnp.bfloat16)
    raw_block = jnp.dot(own_edge, hidden_full, preferred_element_type=jnp.float32)
    enlarged = enlarge(raw_block, vertex_weights)
    projected = jnp.dot(enlarged, proj_next, preferred_element_type=jnp.float32)
    new_corner = passed_along(projected.astype(jnp.bfloat16), "dir", 1)
    partial_gram = jnp.dot(projected.T, projected, precision=lax.Precision.HIGHEST)
    partials = lax.all_to_all(partial_gram, "bond", split_axis=0, concat_axis=0, tiled=True)
    gram = partials.reshape(lax.axis_size("bond"), -1, KEEP).sum(axis=0) / (CHI * D)
    gram = passed_along(gram, "dir", 1)
    return (new_corner[None], gram[None], new_edge[None])


def solution(mesh):
    in_specs = (
        P("dir", "bond", None),
        P("dir", "bond", None),
        P("dir", "bond", None),
        P(),
        P("dir", None, None),
        P("dir", "bond", None),
    )
    out_specs = (P("dir", "bond", None), P("dir", "bond", None), P("dir", "bond", None))
    return jax.shard_map(
        on_device, mesh=mesh, in_specs=in_specs, out_specs=out_specs, check_vma=False
    )
```

```python
import functools

import jax
import jax.numpy as jnp
from jax import lax
from jax.experimental import pallas as pl
from jax.experimental.pallas import tpu as pltpu
from jax.sharding import Mesh, PartitionSpec as P

CHI = 8192
D = 4
PANEL = 512
KEEP = 256
NY = 4
NZ = 8
HALF = PANEL // 2
BATCH_ONE = (0, 1, 7)
BATCH_TWO = (2, 6, 3, 5, 4)


def fetched(block, axis, distance):
    size = lax.axis_size(axis)
    return lax.ppermute(block, axis, [((i + distance) % size, i) for i in range(size)])


def gather_y_then_z(block):
    row = jnp.concatenate(
        [block] + [fetched(block, "y", d) for d in range(1, NY)], axis=0
    )
    pieces = [(row, [(dy, 0) for dy in range(NY)])]
    up = down = row
    for step in range(1, NZ // 2):
        up = fetched(up, "z", 1)
        down = fetched(down, "z", -1)
        pieces.append((up, [(dy, step) for dy in range(NY)]))
        pieces.append((down, [(dy, NZ - step) for dy in range(NY)]))
    middle = row.shape[0] // 2
    top = fetched(up[:middle], "z", 1)
    bottom = fetched(down[middle:], "z", -1)
    pieces.append((top, [(0, NZ // 2), (1, NZ // 2)]))
    pieces.append((bottom, [(2, NZ // 2), (3, NZ // 2)]))
    return pieces


def gather_z_then_y(block):
    column = {0: block}
    up = down = block
    for step in range(1, NZ // 2):
        up = fetched(up, "z", 1)
        down = fetched(down, "z", -1)
        column[step] = up
        column[NZ - step] = down
    column[NZ // 2] = fetched(up, "z", 1)
    pieces = []
    for batch in (BATCH_ONE, BATCH_TWO):
        own = jnp.concatenate([column[dz] for dz in batch], axis=0)
        pieces.append((own, [(0, dz) for dz in batch]))
        for dy in range(1, NY):
            pieces.append((fetched(own, "y", dy), [(dy, dz) for dz in batch]))
    return pieces


def block_of(pos_ref, where):
    dy, dz = where
    y = lax.rem(pos_ref[0] + dy, NY)
    z = lax.rem(pos_ref[1] + dz, NZ)
    return y * NZ + z


def contract_kernel(tables, depth, strides, has_base, swap_rows, pos_ref, *refs):
    n_lhs, n_pieces = len(strides), len(tables)
    lhs_refs = refs[:n_lhs]
    piece_refs = refs[n_lhs : n_lhs + n_pieces]
    rest = refs[n_lhs + n_pieces :]
    base_ref = rest[0] if has_base else None
    out_ref = rest[1 if has_base else 0]
    scratch = rest[(2 if has_base else 1) :]
    slots, sems = scratch[:n_lhs], scratch[n_lhs]
    copies = []
    index = 0
    for table in tables:
        for where in table:
            block = block_of(pos_ref, where)
            for which in range(n_lhs):
                column = block * strides[which]
                if strides[which] == 2:
                    column = column + pos_ref[2]
                start = pl.multiple_of(column * depth, depth)
                copy = pltpu.make_async_copy(
                    lhs_refs[which].at[:, pl.ds(start, depth)],
                    slots[which].at[index],
                    sems.at[which, index],
                )
                copy.start()
                copies.append(copy)
            index += 1
    index = 0
    totals = [None] * n_lhs
    for table, piece_ref in zip(tables, piece_refs):
        for _ in range(len(table) * n_lhs):
            copies.pop(0).wait()
        piece = piece_ref[...]
        for which in range(n_lhs):
            left = jnp.concatenate(
                [slots[which][index + j] for j in range(len(table))], axis=1
            )
            product = jnp.dot(left, piece, preferred_element_type=jnp.float32)
            totals[which] = product if totals[which] is None else totals[which] + product
        index += len(table)
    for which in range(n_lhs):
        rows = slots[which].shape[1]
        total = totals[which]
        if swap_rows:
            place = pos_ref[2] if which == 0 else 1 - pos_ref[2]
            out_ref[pl.ds(pl.multiple_of(place * rows, rows), rows), :] = total
        else:
            if has_base:
                total = total + base_ref[...]
            out_ref[...] = total


def contract(position, lhs, strides, depth, pieces, base=None):
    tables = [table for _, table in pieces]
    arrays = [array for array, _ in pieces]
    count = sum(len(table) for table in tables)
    row_counts = [matrix.shape[0] for matrix in lhs]
    columns = arrays[0].shape[1]
    vmem = pl.BlockSpec(memory_space=pltpu.VMEM)
    extra = [] if base is None else [base]
    total_rows = sum(row_counts)
    grant = 2 * count * depth * (total_rows + columns) + 8 * total_rows * columns * (len(tables) + 2)
    return pl.pallas_call(
        functools.partial(
            contract_kernel, tables, depth, strides, base is not None, len(lhs) > 1
        ),
        out_shape=jax.ShapeDtypeStruct((total_rows, columns), jnp.float32),
        in_specs=[pl.BlockSpec(memory_space=pltpu.SMEM)]
        + [pl.BlockSpec(memory_space=pl.ANY)] * len(lhs)
        + [vmem] * (len(arrays) + len(extra)),
        out_specs=vmem,
        scratch_shapes=[
            pltpu.VMEM((count, rows, depth), jnp.bfloat16) for rows in row_counts
        ]
        + [pltpu.SemaphoreType.DMA((len(lhs), count))],
        compiler_params=pltpu.CompilerParams(vmem_limit_bytes=grant + (8 << 20)),
        cost_estimate=pl.CostEstimate(
            flops=2 * total_rows * columns * depth * count,
            bytes_accessed=2 * count * depth * (total_rows + columns),
            transcendentals=0,
        ),
    )(position, *lhs, *arrays, *extra)


def pick_kernel(pos_ref, corner_ref, out_ref):
    for block in range(NY * NZ):
        start = pl.multiple_of((2 * block + 1 - pos_ref[2]) * 128, 128)
        out_ref[:, block * 128 : (block + 1) * 128] = corner_ref[:, pl.ds(start, 128)]


def partner_columns(position, corner_rows):
    vmem = pl.BlockSpec(memory_space=pltpu.VMEM)
    return pl.pallas_call(
        pick_kernel,
        out_shape=jax.ShapeDtypeStruct((corner_rows.shape[0], CHI // 2), jnp.bfloat16),
        in_specs=[pl.BlockSpec(memory_space=pltpu.SMEM), vmem],
        out_specs=vmem,
        compiler_params=pltpu.CompilerParams(vmem_limit_bytes=16 << 20),
        cost_estimate=pl.CostEstimate(flops=0, bytes_accessed=3 << 20, transcendentals=0),
    )(position, corner_rows)


def finish_kernel(raw_low_ref, raw_high_ref, weight_ref, proj_ref, corner_ref, gram_ref):
    width = PANEL // D
    low, high = raw_low_ref[...], raw_high_ref[...]
    parts = [low[:, :width], low[:, width:], high[:, :width], high[:, width:]]
    mixed = []
    for t in range(D):
        total = None
        for u in range(D):
            term = parts[u] * weight_ref[:, u * D + t : u * D + t + 1]
            total = term if total is None else total + term
        mixed.append(total.astype(jnp.bfloat16))
    enlarged = jnp.concatenate(mixed, axis=1)
    projected = jnp.dot(enlarged, proj_ref[...], preferred_element_type=jnp.float32)
    corner_ref[...] = projected.astype(jnp.bfloat16)
    gram_ref[...] = lax.dot_general(
        projected,
        projected,
        (((0,), (0,)), ((), ())),
        precision=lax.Precision.HIGHEST,
        preferred_element_type=jnp.float32,
    )


def finish(raw_low, raw_high, row_weights, proj):
    vmem = pl.BlockSpec(memory_space=pltpu.VMEM)
    rows = raw_low.shape[0]
    return pl.pallas_call(
        finish_kernel,
        out_shape=(
            jax.ShapeDtypeStruct((rows, KEEP), jnp.bfloat16),
            jax.ShapeDtypeStruct((KEEP, KEEP), jnp.float32),
        ),
        in_specs=[vmem] * 4,
        out_specs=(vmem, vmem),
        compiler_params=pltpu.CompilerParams(vmem_limit_bytes=24 << 20),
        cost_estimate=pl.CostEstimate(
            flops=2 * rows * KEEP * (PANEL + 6 * KEEP),
            bytes_accessed=3 << 20,
            transcendentals=0,
        ),
    )(raw_low, raw_high, row_weights, proj)


def to_previous_direction(block, flip):
    directions = lax.axis_size("dir")
    route = [
        (k * 2 + x, ((k - 1) % directions) * 2 + (1 - x if flip else x))
        for k in range(directions)
        for x in range(2)
    ]
    return lax.ppermute(block, ("dir", "xh"), route)


def on_device(corner_mat, edge_mat, edge_panel, vertex_weights, projector, edge_projector):
    corner_rows = corner_mat[0]
    own_edge = edge_mat[0]
    panel_rows = edge_panel[0]
    xh = lax.axis_index("xh")
    position = jnp.stack([lax.axis_index("y"), lax.axis_index("z"), xh]).astype(jnp.int32)

    partner_corner = fetched(partner_columns(position, corner_rows), "xh", 1)
    panel_pieces = (
        gather_y_then_z(panel_rows[:, :HALF]),
        gather_z_then_y(panel_rows[:, HALF:]),
    )
    edge_proj_rows = lax.all_to_all(
        edge_projector[0].T, ("y", "z"), split_axis=0, concat_axis=1, tiled=True
    )
    proj_next = fetched(projector[0], "dir", 1)
    row_weights = jnp.tile(vertex_weights.reshape(D, D * D), (own_edge.shape[0] // D, 1))

    raws = []
    edge_parts = []
    for chain, gather in enumerate((gather_y_then_z, gather_z_then_y)):
        pieces = panel_pieces[chain]
        partial = contract(position, (corner_rows, partner_corner), (2, 1), 128, pieces)
        hidden = (
            to_previous_direction(partial, False) + to_previous_direction(partial, True)
        ).astype(jnp.bfloat16)
        hidden_pieces = gather(hidden)
        early = 5
        raw = contract(position, (own_edge,), (1,), 256, hidden_pieces[:early])
        raw = contract(position, (own_edge,), (1,), 256, hidden_pieces[early:], raw)
        raws.append(raw)
        padded = jnp.pad(edge_proj_rows, ((0, 8), (0, 0)))
        edge_parts.append(contract(position, (padded,), (1,), 128, pieces))

    edge_part = jnp.concatenate(edge_parts, axis=1)[:8].reshape(2, 4, PANEL)
    edge_other = fetched(lax.dynamic_index_in_dim(edge_part, 1 - xh, 0, False), "xh", 1)
    new_edge = (
        lax.dynamic_index_in_dim(edge_part, xh, 0, False) + edge_other
    ).astype(jnp.bfloat16)

    corner_here, partial_gram = finish(raws[0], raws[1], row_weights, proj_next)
    partials = lax.all_to_all(
        partial_gram, ("y", "z", "xh"), split_axis=0, concat_axis=0, tiled=True
    )
    gram = partials.reshape(-1, 4, KEEP).sum(axis=0) / (CHI * D)
    new_corner = fetched(corner_here, "dir", -1)
    gram = fetched(gram, "dir", -1)
    return (new_corner[None], gram[None], new_edge[None])


def solution(mesh):
    fine = Mesh(mesh.devices.reshape(4, NY, NZ, 2), ("dir", "y", "z", "xh"))
    rows = P("dir", ("y", "z", "xh"), None)
    in_specs = (rows, rows, rows, P(), P("dir", None, None), rows)
    return jax.shard_map(
        on_device, mesh=fine, in_specs=in_specs, out_specs=(rows, rows, rows), check_vma=False
    )
```

```python
import jax
import jax.numpy as jnp
from jax import lax
from jax.experimental import pallas as pl
from jax.experimental.pallas import tpu as pltpu
from jax.sharding import Mesh, PartitionSpec as P

CHI = 8192
D = 4
PANEL = 512
KEEP = 256
NY = 4
NZ = 8
HALF = PANEL // 2
GRANT = 52 << 20
EDGE_ROWS = CHI * D // 64
DEPTH = 256


def fetched(block, axis, distance):
    size = lax.axis_size(axis)
    return lax.ppermute(block, axis, [((i + distance) % size, i) for i in range(size)])


def tied(*values):
    return lax.optimization_barrier(values)


class Product:
    def __init__(self, pieces):
        self.pieces = pieces
        self.count = sum(len(table) for _, _, table in pieces)

    def scratch(self):
        return [
            pltpu.VMEM((self.count, EDGE_ROWS, DEPTH), jnp.bfloat16),
            pltpu.VMEM((self.count * DEPTH, HALF), jnp.bfloat16),
            pltpu.SemaphoreType.DMA((self.count,)),
            pltpu.SemaphoreType.DMA((len(self.pieces),)),
        ]

    def start(self, pos_ref, edge_ref, piece_refs, scratch):
        slots, held, edge_sems, piece_sems = scratch
        copies = []
        index = 0
        for p, ((_, first, table), piece_ref) in enumerate(zip(self.pieces, piece_refs)):
            size = len(table) * DEPTH
            group = [
                pltpu.make_async_copy(
                    piece_ref.at[pl.ds(first, size)],
                    held.at[pl.ds(index * DEPTH, size)],
                    piece_sems.at[p],
                )
            ]
            for dy, dz in table:
                block = lax.rem(pos_ref[0] + dy, NY) * NZ + lax.rem(pos_ref[1] + dz, NZ)
                group.append(
                    pltpu.make_async_copy(
                        edge_ref.at[:, pl.ds(pl.multiple_of(block * DEPTH, DEPTH), DEPTH)],
                        slots.at[index],
                        edge_sems.at[index],
                    )
                )
                index += 1
            for copy in group:
                copy.start()
            copies.append(group)
        return copies

    def finish(self, copies, scratch):
        slots, held = scratch[:2]
        total = None
        index = 0
        for (_, _, table), group in zip(self.pieces, copies):
            for copy in group:
                copy.wait()
            piece = held[index * DEPTH : (index + len(table)) * DEPTH, :]
            left = jnp.concatenate([slots[index + j] for j in range(len(table))], axis=1)
            product = jnp.dot(left, piece, preferred_element_type=jnp.float32)
            total = product if total is None else total + product
            index += len(table)
        return total


def run_products(position, edge_rows, products, body, out_shape, extra=()):
    arrays = []
    for product in products:
        for array, _, _ in product.pieces:
            if all(array is not other for other in arrays):
                arrays.append(array)
    places = [
        [[array is other for other in arrays].index(True) for array, _, _ in product.pieces]
        for product in products
    ]
    sizes = [len(product.scratch()) for product in products]
    outs = len(out_shape)

    def kernel(pos_ref, edge_ref, *refs):
        array_refs, refs = refs[: len(arrays)], refs[len(arrays) :]
        extra_refs, refs = refs[: len(extra)], refs[len(extra) :]
        out_refs, refs = refs[:outs], refs[outs:]
        scratches = []
        for size in sizes:
            scratches.append(refs[:size])
            refs = refs[size:]
        started = [
            product.start(pos_ref, edge_ref, [array_refs[i] for i in place], scratch)
            for product, place, scratch in zip(products, places, scratches)
        ]
        totals = [
            product.finish(copies, scratch)
            for product, copies, scratch in zip(products, started, scratches)
        ]
        body(totals, extra_refs, out_refs)

    vmem = pl.BlockSpec(memory_space=pltpu.VMEM)
    hbm = pl.BlockSpec(memory_space=pl.ANY)
    depth = sum(product.count for product in products) * DEPTH
    return pl.pallas_call(
        kernel,
        out_shape=out_shape,
        in_specs=[pl.BlockSpec(memory_space=pltpu.SMEM)]
        + [hbm] * (1 + len(arrays))
        + [vmem] * len(extra),
        out_specs=(vmem,) * outs,
        scratch_shapes=[shape for product in products for shape in product.scratch()],
        compiler_params=pltpu.CompilerParams(vmem_limit_bytes=GRANT),
        cost_estimate=pl.CostEstimate(
            flops=2 * EDGE_ROWS * HALF * depth,
            bytes_accessed=2 * (EDGE_ROWS + HALF) * depth,
            transcendentals=0,
        ),
    )(position, edge_rows, *arrays, *extra)


def raw_body(totals, extra_refs, out_refs):
    for chain in range(2):
        total = totals[chain]
        if extra_refs:
            total = total + extra_refs[chain][...]
        out_refs[chain][...] = total


def raw_products(position, edge_rows, low_pieces, high_pieces, base=()):
    return run_products(
        position,
        edge_rows,
        [Product(low_pieces), Product(high_pieces)],
        raw_body,
        (jax.ShapeDtypeStruct((EDGE_ROWS, HALF), jnp.float32),) * 2,
        tuple(base),
    )


def finish_body(totals, extra_refs, out_refs):
    low_ref, high_ref, weight_ref, proj_ref = extra_refs
    corner_ref, gram_ref = out_refs
    width = PANEL // D
    low = low_ref[...] + totals[0]
    high = high_ref[...] + totals[1]
    parts = [low[:, :width], low[:, width:], high[:, :width], high[:, width:]]
    mixed = []
    for t in range(D):
        total = None
        for u in range(D):
            term = parts[u] * weight_ref[:, u * D + t : u * D + t + 1]
            total = term if total is None else total + term
        mixed.append(total.astype(jnp.bfloat16))
    enlarged = jnp.concatenate(mixed, axis=1)
    projected = jnp.dot(enlarged, proj_ref[...], preferred_element_type=jnp.float32)
    corner_ref[...] = projected.astype(jnp.bfloat16)
    gram_ref[...] = lax.dot_general(
        projected,
        projected,
        (((0,), (0,)), ((), ())),
        precision=lax.Precision.HIGHEST,
        preferred_element_type=jnp.float32,
    )


def sort_kernel(corner_ref, out_ref):
    for y in range(NY):
        for z in range(NZ):
            for x in range(2):
                block = ((y * NZ + z) * 2 + x) * 128
                out_ref[y * 2 + x, :, z * 128 : (z + 1) * 128] = corner_ref[:, block : block + 128]


def sorted_columns(corner_rows):
    vmem = pl.BlockSpec(memory_space=pltpu.VMEM)
    return pl.pallas_call(
        sort_kernel,
        out_shape=jax.ShapeDtypeStruct((NY * 2, 128, NZ * 128), jnp.bfloat16),
        in_specs=[vmem],
        out_specs=vmem,
        compiler_params=pltpu.CompilerParams(vmem_limit_bytes=16 << 20),
        cost_estimate=pl.CostEstimate(flops=0, bytes_accessed=4 << 20, transcendentals=0),
    )(corner_rows)


def partial_kernel(pos_ref, corner_ref, *refs):
    piece_refs, out_ref, panel, edges = refs[:NZ], refs[NZ], refs[NZ + 1], refs[NZ + 2]
    for dz, piece_ref in enumerate(piece_refs):
        start = pl.multiple_of(lax.rem(pos_ref[1] + dz, NZ) * 128, 128)
        panel[pl.ds(start, 128), :] = piece_ref[...]
    held = panel[:, :PANEL]
    edges[...] = lax.dot_general(
        panel[:, PANEL:], held, (((0,), (0,)), ((), ())), preferred_element_type=jnp.float32
    )
    corner = corner_ref[...].reshape(NY * 2 * 128, NZ * 128)
    product = jnp.dot(corner, held, preferred_element_type=jnp.float32).astype(jnp.bfloat16)
    for group in range(NY * 2):
        out_ref[group, :128] = product[group * 128 : (group + 1) * 128]
        start = pl.multiple_of((group // 2) * NZ * 8 + pos_ref[1] * 8, 8)
        rows = edges[pl.ds(start, 8), :]
        out_ref[group, 128:] = jnp.concatenate([rows, jnp.zeros_like(rows)], axis=0).astype(
            jnp.bfloat16
        )


def partial_products(position, corner_part, pieces):
    vmem = pl.BlockSpec(memory_space=pltpu.VMEM)
    rows = 128 + 16
    return pl.pallas_call(
        partial_kernel,
        out_shape=jax.ShapeDtypeStruct((NY * 2, rows, PANEL), jnp.bfloat16),
        in_specs=[pl.BlockSpec(memory_space=pltpu.SMEM)] + [vmem] * (1 + NZ),
        out_specs=vmem,
        scratch_shapes=[
            pltpu.VMEM((NZ * 128, PANEL + KEEP), jnp.bfloat16),
            pltpu.VMEM((KEEP, PANEL), jnp.float32),
        ],
        compiler_params=pltpu.CompilerParams(vmem_limit_bytes=24 << 20),
        cost_estimate=pl.CostEstimate(
            flops=2 * NY * 2 * rows * NZ * 128 * PANEL, bytes_accessed=4 << 20, transcendentals=0
        ),
    )(position, corner_part, *pieces)


def to_direction(block, shift, flip):
    directions = lax.axis_size("dir")
    route = [
        (k * 2 + x, ((k + shift) % directions) * 2 + (1 - x if flip else x))
        for k in range(directions)
        for x in range(2)
    ]
    return lax.ppermute(block, ("dir", "xh"), route)


def half_rows(block, which):
    return lax.dynamic_slice_in_dim(block, which * 4, 4, 0)


def on_device(corner_mat, edge_mat, edge_panel, vertex_weights, projector, edge_projector):
    corner_rows = corner_mat[0]
    own_edge = edge_mat[0]
    panel_rows = edge_panel[0]
    xh = lax.axis_index("xh")
    position = jnp.stack([lax.axis_index("y"), lax.axis_index("z")]).astype(jnp.int32)

    corner_part = lax.all_to_all(
        sorted_columns(corner_rows), ("y", "xh"), split_axis=0, concat_axis=0, tiled=True
    )
    up = down = jnp.concatenate([panel_rows, edge_projector[0]], axis=1)
    panel_part = {0: up}
    for step in range(1, NZ // 2):
        up, down = fetched(up, "z", 1), fetched(down, "z", -1)
        panel_part[step], panel_part[NZ - step] = up, down
    panel_part[NZ // 2] = fetched(up, "z", 1)

    partials = lax.all_to_all(
        partial_products(position, corner_part, [panel_part[dz] for dz in range(NZ)]),
        ("y", "xh"),
        split_axis=0,
        concat_axis=0,
        tiled=True,
    )
    sums = partials.astype(jnp.float32).sum(axis=0).astype(jnp.bfloat16)
    hidden, new_edge = sums[:128], half_rows(sums[128:136], xh)

    same = to_direction(hidden, -1, False)
    other = to_direction(hidden, -1, True)
    block = jnp.where(
        xh == 0, jnp.concatenate([same, other], 0), jnp.concatenate([other, same], 0)
    )
    left, right = tied(block[:, :HALF], block[:, HALF:])
    proj_next = fetched(projector[0], "dir", 1)
    row_weights = jnp.tile(vertex_weights.reshape(D, D * D), (EDGE_ROWS // D, 1))

    cut = NY * DEPTH

    def all_y(dz):
        return [(dy, dz) for dy in range(NY)]

    def over_y(block):
        return [fetched(block, "y", dy) for dy in (1, 3, 2)]

    def pieces_y(arrays, dzs):
        return [(array, 0, [(dy, dz) for dz in dzs]) for array, dy in zip(arrays, (1, 3, 2))]

    def ring(up, down):
        return fetched(up, "z", 1), fetched(down, "z", -1)

    near = over_y(left)
    up, down = ring(right, right)
    near, up, down = tied(near, up, down)

    row = jnp.concatenate([left, near[0], near[2], near[1]], axis=0)
    first = jnp.concatenate([right, up, down], axis=0)
    up, down = jnp.concatenate([row, up], axis=0), jnp.concatenate([row, down], axis=0)
    raws = raw_products(
        position, own_edge, [(row, 0, all_y(0))], [(first, 0, [(0, 0), (0, 1), (0, 7)])]
    )
    up, down = ring(up, down)
    batch = over_y(first)
    up, down, batch, raws = tied(up, down, batch, raws)

    second = jnp.concatenate([up[cut:], down[cut:]], axis=0)
    raws = raw_products(
        position,
        own_edge,
        [(up, 0, all_y(1)), (down, 0, all_y(7))],
        [(second, 0, [(0, 2), (0, 6)])] + pieces_y(batch, (0, 1, 7)),
        raws,
    )
    up, down = ring(up, down)
    batch = over_y(second)
    up, down, batch, raws = tied(up, down, batch, raws)

    third = jnp.concatenate([up[cut:], down[cut:]], axis=0)
    raws = raw_products(
        position,
        own_edge,
        [(up, 0, all_y(2)), (down, 0, all_y(6))],
        [(third, 0, [(0, 3), (0, 5)])] + pieces_y(batch, (2, 6)),
        raws,
    )
    up, down = ring(up, down)
    batch = over_y(third)
    up, down, batch, raws = tied(up, down, batch, raws)

    fourth = up[cut:]
    raws = raw_products(
        position,
        own_edge,
        [(up, 0, all_y(3)), (down, 0, all_y(5))],
        [(fourth, 0, [(0, 4)])] + pieces_y(batch, (3, 5)),
        raws,
    )
    top, bottom = ring(up[: cut // 2], down[cut // 2 : cut])
    batch = over_y(fourth)
    corner_here, partial_gram = run_products(
        position,
        own_edge,
        [
            Product([(top, 0, all_y(4)[:2]), (bottom, 0, all_y(4)[2:])]),
            Product(pieces_y(batch, (4,))),
        ],
        finish_body,
        (
            jax.ShapeDtypeStruct((EDGE_ROWS, KEEP), jnp.bfloat16),
            jax.ShapeDtypeStruct((KEEP, KEEP), jnp.float32),
        ),
        (raws[0], raws[1], row_weights, proj_next),
    )
    new_corner = fetched(corner_here, "dir", -1)
    partials = lax.all_to_all(
        partial_gram.reshape(NY * NZ, 8, KEEP), ("y", "z"), split_axis=0, concat_axis=0, tiled=True
    )
    gram_part = partials.sum(axis=0)
    gram = (
        to_direction(half_rows(gram_part, xh), 1, False)
        + to_direction(half_rows(gram_part, 1 - xh), 1, True)
    ) / (CHI * D)
    return (new_corner[None], gram[None], new_edge[None])


def solution(mesh):
    fine = Mesh(mesh.devices.reshape(4, NY, NZ, 2), ("dir", "y", "z", "xh"))
    rows = P("dir", ("y", "z", "xh"), None)
    in_specs = (rows, rows, rows, P(), P("dir", None, None), rows)
    return jax.shard_map(
        on_device, mesh=fine, in_specs=in_specs, out_specs=(rows, rows, rows), check_vma=False
    )
```

```python
import jax
import jax.numpy as jnp
from jax import lax
from jax.experimental import pallas as pl
from jax.experimental.pallas import tpu as pltpu
from jax.sharding import Mesh, PartitionSpec as P

CHI = 8192
D = 4
PANEL = 512
KEEP = 256
NY = 4
NZ = 8
HALF = PANEL // 2
GRANT = 14 << 20
CUT_GRANT = 16 << 20
EDGE_ROWS = CHI * D // 64
DEPTH = 256


def fetched(block, axis, distance):
    size = lax.axis_size(axis)
    return lax.ppermute(block, axis, [((i + distance) % size, i) for i in range(size)])


def tied(*values):
    return lax.optimization_barrier(values)


class Product:
    def __init__(self, pieces):
        self.pieces = pieces
        self.count = sum(len(table) for _, _, table in pieces)

    def run(self, edge_refs, piece_refs):
        total = None
        for (_, first, table), piece_ref in zip(self.pieces, piece_refs):
            piece = piece_ref[first : first + len(table) * DEPTH, :]
            left = jnp.concatenate([edge_refs[dz][dy] for dy, dz in table], axis=1)
            product = jnp.dot(left, piece, preferred_element_type=jnp.float32)
            total = product if total is None else total + product
        return total


def run_products(edge_blocks, products, body, out_shape, extra=()):
    arrays, needed = [], []
    for product in products:
        for array, _, table in product.pieces:
            if all(array is not other for other in arrays):
                arrays.append(array)
            needed += [dz for _, dz in table if dz not in needed]
    places = [
        [[array is other for other in arrays].index(True) for array, _, _ in product.pieces]
        for product in products
    ]
    outs = len(out_shape)

    def kernel(*refs):
        edge_refs, refs = dict(zip(needed, refs)), refs[len(needed) :]
        array_refs, refs = refs[: len(arrays)], refs[len(arrays) :]
        extra_refs, out_refs = refs[: len(extra)], refs[len(extra) :]
        totals = [
            product.run(edge_refs, [array_refs[i] for i in place])
            for product, place in zip(products, places)
        ]
        body(totals, extra_refs, out_refs)

    vmem = pl.BlockSpec(memory_space=pltpu.VMEM)
    count = sum(product.count for product in products)
    return pl.pallas_call(
        kernel,
        out_shape=out_shape,
        in_specs=[vmem] * (len(needed) + len(arrays) + len(extra)),
        out_specs=(vmem,) * outs,
        compiler_params=pltpu.CompilerParams(vmem_limit_bytes=GRANT),
        cost_estimate=pl.CostEstimate(
            flops=2 * EDGE_ROWS * HALF * count * DEPTH,
            bytes_accessed=2 * (EDGE_ROWS + HALF) * count * DEPTH,
            transcendentals=0,
        ),
    )(*[edge_blocks[dz] for dz in needed], *arrays, *extra)


def cut_kernel(pos_ref, edge_ref, *refs):
    out_refs, sems = refs[:NZ], refs[NZ]
    copies = []
    for dz in range(NZ):
        for dy in range(NY):
            block = lax.rem(pos_ref[0] + dy, NY) * NZ + lax.rem(pos_ref[1] + dz, NZ)
            copies.append(
                pltpu.make_async_copy(
                    edge_ref.at[:, pl.ds(pl.multiple_of(block * DEPTH, DEPTH), DEPTH)],
                    out_refs[dz].at[dy],
                    sems.at[dz, dy],
                )
            )
    for copy in copies:
        copy.start()
    for copy in copies:
        copy.wait()


def cut_edge(position, edge_rows):
    vmem = pl.BlockSpec(memory_space=pltpu.VMEM)
    return pl.pallas_call(
        cut_kernel,
        out_shape=(jax.ShapeDtypeStruct((NY, EDGE_ROWS, DEPTH), jnp.bfloat16),) * NZ,
        in_specs=[pl.BlockSpec(memory_space=pltpu.SMEM), pl.BlockSpec(memory_space=pl.ANY)],
        out_specs=(vmem,) * NZ,
        scratch_shapes=[pltpu.SemaphoreType.DMA((NZ, NY))],
        compiler_params=pltpu.CompilerParams(vmem_limit_bytes=CUT_GRANT),
        cost_estimate=pl.CostEstimate(flops=0, bytes_accessed=16 << 20, transcendentals=0),
    )(position, edge_rows)


def raw_body(totals, extra_refs, out_refs):
    for chain in range(2):
        total = totals[chain]
        if extra_refs:
            total = total + extra_refs[chain][...]
        out_refs[chain][...] = total


def raw_products(edge_blocks, low_pieces, high_pieces, base=()):
    return run_products(
        edge_blocks,
        [Product(low_pieces), Product(high_pieces)],
        raw_body,
        (jax.ShapeDtypeStruct((EDGE_ROWS, HALF), jnp.float32),) * 2,
        tuple(base),
    )


def finish_body(totals, extra_refs, out_refs):
    low_ref, high_ref, weight_ref, proj_ref = extra_refs
    corner_ref, gram_ref = out_refs
    width = PANEL // D
    low = low_ref[...] + totals[0]
    high = high_ref[...] + totals[1]
    parts = [low[:, :width], low[:, width:], high[:, :width], high[:, width:]]
    mixed = []
    for t in range(D):
        total = None
        for u in range(D):
            term = parts[u] * weight_ref[:, u * D + t : u * D + t + 1]
            total = term if total is None else total + term
        mixed.append(total.astype(jnp.bfloat16))
    enlarged = jnp.concatenate(mixed, axis=1)
    projected = jnp.dot(enlarged, proj_ref[...], preferred_element_type=jnp.float32)
    corner_ref[...] = projected.astype(jnp.bfloat16)
    gram_ref[...] = lax.dot_general(
        projected,
        projected,
        (((0,), (0,)), ((), ())),
        precision=lax.Precision.HIGHEST,
        preferred_element_type=jnp.float32,
    )


def sort_kernel(corner_ref, out_ref):
    for y in range(NY):
        for z in range(NZ):
            for x in range(2):
                block = ((y * NZ + z) * 2 + x) * 128
                out_ref[y * 2 + x, :, z * 128 : (z + 1) * 128] = corner_ref[:, block : block + 128]


def sorted_columns(corner_rows):
    vmem = pl.BlockSpec(memory_space=pltpu.VMEM)
    return pl.pallas_call(
        sort_kernel,
        out_shape=jax.ShapeDtypeStruct((NY * 2, 128, NZ * 128), jnp.bfloat16),
        in_specs=[vmem],
        out_specs=vmem,
        compiler_params=pltpu.CompilerParams(vmem_limit_bytes=16 << 20),
        cost_estimate=pl.CostEstimate(flops=0, bytes_accessed=4 << 20, transcendentals=0),
    )(corner_rows)


def partial_kernel(pos_ref, corner_ref, *refs):
    piece_refs, out_refs = refs[:NZ], refs[NZ : NZ + NY]
    panel, edges, products = refs[NZ + NY :]
    for dz, piece_ref in enumerate(piece_refs):
        start = pl.multiple_of(lax.rem(pos_ref[1] + dz, NZ) * 128, 128)
        panel[pl.ds(start, 128), :] = piece_ref[...]
    held = panel[:, :PANEL]
    edges[...] = lax.dot_general(
        panel[:, PANEL:], held, (((0,), (0,)), ((), ())), preferred_element_type=jnp.float32
    )
    corner = corner_ref[...].reshape(NY * 2 * 128, NZ * 128)
    products[...] = jnp.dot(corner, held, preferred_element_type=jnp.float32).astype(jnp.bfloat16)
    for dy, out_ref in enumerate(out_refs):
        y = lax.rem(pos_ref[0] + dy, NY)
        out_ref[:DEPTH] = products[pl.ds(pl.multiple_of(y * DEPTH, DEPTH), DEPTH), :]
        start = pl.multiple_of((y * NZ + pos_ref[1]) * 8, 8)
        rows = edges[pl.ds(start, 8), :]
        high = rows.astype(jnp.bfloat16).astype(jnp.float32)
        out_ref[DEPTH:] = jnp.concatenate([high, rows - high], axis=0).astype(jnp.bfloat16)


def partial_products(position, corner_part, pieces):
    vmem = pl.BlockSpec(memory_space=pltpu.VMEM)
    rows = DEPTH + 16
    return pl.pallas_call(
        partial_kernel,
        out_shape=(jax.ShapeDtypeStruct((rows, PANEL), jnp.bfloat16),) * NY,
        in_specs=[pl.BlockSpec(memory_space=pltpu.SMEM)] + [vmem] * (1 + NZ),
        out_specs=(vmem,) * NY,
        scratch_shapes=[
            pltpu.VMEM((NZ * 128, PANEL + KEEP), jnp.bfloat16),
            pltpu.VMEM((KEEP, PANEL), jnp.float32),
            pltpu.VMEM((NY * DEPTH, PANEL), jnp.bfloat16),
        ],
        compiler_params=pltpu.CompilerParams(vmem_limit_bytes=24 << 20),
        cost_estimate=pl.CostEstimate(
            flops=2 * NY * rows * NZ * 128 * PANEL, bytes_accessed=4 << 20, transcendentals=0
        ),
    )(position, corner_part, *pieces)


def to_direction(block, shift, flip):
    directions = lax.axis_size("dir")
    route = [
        (k * 2 + x, ((k + shift) % directions) * 2 + (1 - x if flip else x))
        for k in range(directions)
        for x in range(2)
    ]
    return lax.ppermute(block, ("dir", "xh"), route)


def half_rows(block, which):
    return lax.dynamic_slice_in_dim(block, which * 4, 4, 0)


def on_device(corner_mat, edge_mat, edge_panel, vertex_weights, projector, edge_projector):
    corner_rows = corner_mat[0]
    panel_rows = edge_panel[0]
    xh = lax.axis_index("xh")
    position = jnp.stack([lax.axis_index("y"), lax.axis_index("z")]).astype(jnp.int32)
    edge_blocks = cut_edge(position, edge_mat[0])

    corner_part = lax.all_to_all(
        sorted_columns(corner_rows), ("y", "xh"), split_axis=0, concat_axis=0, tiled=True
    )
    up = down = jnp.concatenate([panel_rows, edge_projector[0]], axis=1)
    panel_part = {0: up}
    for step in range(1, NZ // 2):
        up, down = fetched(up, "z", 1), fetched(down, "z", -1)
        panel_part[step], panel_part[NZ - step] = up, down
    panel_part[NZ // 2] = fetched(up, "z", 1)

    mine, *others = partial_products(
        position, corner_part, [panel_part[dz] for dz in range(NZ)]
    )
    arrived = [fetched(others[dy - 1], "y", -dy) for dy in range(1, NY)]
    arrived, edge_blocks = tied(arrived, edge_blocks)
    sums = mine.astype(jnp.float32)
    for part in arrived:
        sums = sums + part.astype(jnp.float32)
    edge_part = sums[DEPTH : DEPTH + 8] + sums[DEPTH + 8 :]
    partial = sums[:DEPTH].astype(jnp.bfloat16)
    same, other = to_direction(partial, -1, False), to_direction(partial, -1, True)
    block = (same.astype(jnp.float32) + other.astype(jnp.float32)).astype(jnp.bfloat16)
    left, right = tied(block[:, :HALF], block[:, HALF:])
    proj_next = fetched(projector[0], "dir", 1)
    row_weights = jnp.tile(vertex_weights.reshape(D, D * D), (EDGE_ROWS // D, 1))

    cut = NY * DEPTH

    def all_y(dz):
        return [(dy, dz) for dy in range(NY)]

    def over_y(block):
        return [fetched(block, "y", dy) for dy in (1, 3, 2)]

    def pieces_y(arrays, dzs):
        return [(array, 0, [(dy, dz) for dz in dzs]) for array, dy in zip(arrays, (1, 3, 2))]

    def ring(up, down):
        return fetched(up, "z", 1), fetched(down, "z", -1)

    near = over_y(left)
    up, down = ring(right, right)
    near, up, down = tied(near, up, down)

    row = jnp.concatenate([left, near[0], near[2], near[1]], axis=0)
    first = jnp.concatenate([right, up, down], axis=0)
    up, down = jnp.concatenate([row, up], axis=0), jnp.concatenate([row, down], axis=0)
    raws = raw_products(
        edge_blocks, [(row, 0, all_y(0))], [(first, 0, [(0, 0), (0, 1), (0, 7)])]
    )
    up, down = ring(up, down)
    batch = over_y(first)
    up, down, batch, raws = tied(up, down, batch, raws)

    second = jnp.concatenate([up[cut:], down[cut:]], axis=0)
    raws = raw_products(
        edge_blocks,
        [(up, 0, all_y(1)), (down, 0, all_y(7))],
        [(second, 0, [(0, 2), (0, 6)])] + pieces_y(batch, (0, 1, 7)),
        raws,
    )
    up, down = ring(up, down)
    batch = over_y(second)
    up, down, batch, raws = tied(up, down, batch, raws)

    third = jnp.concatenate([up[cut:], down[cut:]], axis=0)
    raws = raw_products(
        edge_blocks,
        [(up, 0, all_y(2)), (down, 0, all_y(6))],
        [(third, 0, [(0, 3), (0, 5)])] + pieces_y(batch, (2, 6)),
        raws,
    )
    up, down = ring(up, down)
    batch = over_y(third)
    up, down, batch, raws = tied(up, down, batch, raws)

    fourth = up[cut:]
    raws = raw_products(
        edge_blocks,
        [(up, 0, all_y(3)), (down, 0, all_y(5))],
        [(fourth, 0, [(0, 4)])] + pieces_y(batch, (3, 5)),
        raws,
    )
    up, down, fourth, raws = tied(up, down, fourth, raws)
    top, bottom = ring(up[: cut // 2], down[cut // 2 : cut])
    batch = over_y(fourth)
    corner_here, partial_gram = run_products(
        edge_blocks,
        [
            Product([(top, 0, all_y(4)[:2]), (bottom, 0, all_y(4)[2:])]),
            Product(pieces_y(batch, (4,))),
        ],
        finish_body,
        (
            jax.ShapeDtypeStruct((EDGE_ROWS, KEEP), jnp.bfloat16),
            jax.ShapeDtypeStruct((KEEP, KEEP), jnp.float32),
        ),
        (raws[0], raws[1], row_weights, proj_next),
    )
    edge_part, corner_here = tied(edge_part, corner_here)
    edge_other = fetched(half_rows(edge_part, 1 - xh), "xh", 1)
    new_edge = (half_rows(edge_part, xh) + edge_other).astype(jnp.bfloat16)
    new_corner = fetched(corner_here, "dir", -1)
    partials = lax.all_to_all(
        partial_gram.reshape(NY * NZ, 8, KEEP), ("y", "z"), split_axis=0, concat_axis=0, tiled=True
    )
    gram_part = partials.sum(axis=0)
    gram = (
        to_direction(half_rows(gram_part, xh), 1, False)
        + to_direction(half_rows(gram_part, 1 - xh), 1, True)
    ) / (CHI * D)
    return (new_corner[None], gram[None], new_edge[None])


def solution(mesh):
    fine = Mesh(mesh.devices.reshape(4, NY, NZ, 2), ("dir", "y", "z", "xh"))
    rows = P("dir", ("y", "z", "xh"), None)
    in_specs = (rows, rows, rows, P(), P("dir", None, None), rows)
    return jax.shard_map(
        on_device, mesh=fine, in_specs=in_specs, out_specs=(rows, rows, rows), check_vma=False
    )
```

```python
import jax
import jax.numpy as jnp
from jax import lax
from jax.experimental import pallas as pl
from jax.experimental.pallas import tpu as pltpu
from jax.sharding import Mesh, PartitionSpec as P

CHI = 8192
D = 4
PANEL = 512
KEEP = 256
NY = 4
NZ = 8
HALF = PANEL // 2
GRANT = 14 << 20
CUT_GRANT = 16 << 20
EDGE_ROWS = CHI * D // 64
DEPTH = 256


def fetched(block, axis, distance):
    size = lax.axis_size(axis)
    return lax.ppermute(block, axis, [((i + distance) % size, i) for i in range(size)])


def tied(*values):
    return lax.optimization_barrier(values)


class Product:
    def __init__(self, pieces):
        self.pieces = pieces
        self.count = sum(len(table) for _, _, table in pieces)

    def run(self, edge_refs, piece_refs):
        total = None
        for (_, first, table), piece_ref in zip(self.pieces, piece_refs):
            piece = piece_ref[first : first + len(table) * DEPTH, :]
            left = jnp.concatenate([edge_refs[dz][dy] for dy, dz in table], axis=1)
            product = jnp.dot(left, piece, preferred_element_type=jnp.float32)
            total = product if total is None else total + product
        return total


def run_products(edge_blocks, products, body, out_shape, extra=()):
    arrays, needed = [], []
    for product in products:
        for array, _, table in product.pieces:
            if all(array is not other for other in arrays):
                arrays.append(array)
            needed += [dz for _, dz in table if dz not in needed]
    places = [
        [[array is other for other in arrays].index(True) for array, _, _ in product.pieces]
        for product in products
    ]
    outs = len(out_shape)

    def kernel(*refs):
        edge_refs, refs = dict(zip(needed, refs)), refs[len(needed) :]
        array_refs, refs = refs[: len(arrays)], refs[len(arrays) :]
        extra_refs, out_refs = refs[: len(extra)], refs[len(extra) :]
        totals = [
            product.run(edge_refs, [array_refs[i] for i in place])
            for product, place in zip(products, places)
        ]
        body(totals, extra_refs, out_refs)

    vmem = pl.BlockSpec(memory_space=pltpu.VMEM)
    count = sum(product.count for product in products)
    return pl.pallas_call(
        kernel,
        out_shape=out_shape,
        in_specs=[vmem] * (len(needed) + len(arrays) + len(extra)),
        out_specs=(vmem,) * outs,
        compiler_params=pltpu.CompilerParams(vmem_limit_bytes=GRANT),
        cost_estimate=pl.CostEstimate(
            flops=2 * EDGE_ROWS * HALF * count * DEPTH,
            bytes_accessed=2 * (EDGE_ROWS + HALF) * count * DEPTH,
            transcendentals=0,
        ),
    )(*[edge_blocks[dz] for dz in needed], *arrays, *extra)


def cut_kernel(pos_ref, edge_ref, *refs):
    out_refs, sems = refs[:NZ], refs[NZ]
    copies = []
    for dz in range(NZ):
        for dy in range(NY):
            block = lax.rem(pos_ref[0] + dy, NY) * NZ + lax.rem(pos_ref[1] + dz, NZ)
            copies.append(
                pltpu.make_async_copy(
                    edge_ref.at[:, pl.ds(pl.multiple_of(block * DEPTH, DEPTH), DEPTH)],
                    out_refs[dz].at[dy],
                    sems.at[dz, dy],
                )
            )
    for copy in copies:
        copy.start()
    for copy in copies:
        copy.wait()


def cut_edge(position, edge_rows):
    vmem = pl.BlockSpec(memory_space=pltpu.VMEM)
    return pl.pallas_call(
        cut_kernel,
        out_shape=(jax.ShapeDtypeStruct((NY, EDGE_ROWS, DEPTH), jnp.bfloat16),) * NZ,
        in_specs=[pl.BlockSpec(memory_space=pltpu.SMEM), pl.BlockSpec(memory_space=pl.ANY)],
        out_specs=(vmem,) * NZ,
        scratch_shapes=[pltpu.SemaphoreType.DMA((NZ, NY))],
        compiler_params=pltpu.CompilerParams(vmem_limit_bytes=CUT_GRANT),
        cost_estimate=pl.CostEstimate(flops=0, bytes_accessed=16 << 20, transcendentals=0),
    )(position, edge_rows)


def raw_body(totals, extra_refs, out_refs):
    for chain in range(2):
        total = totals[chain]
        if extra_refs:
            total = total + extra_refs[chain][...]
        out_refs[chain][...] = total


def raw_products(edge_blocks, low_pieces, high_pieces, base=()):
    return run_products(
        edge_blocks,
        [Product(low_pieces), Product(high_pieces)],
        raw_body,
        (jax.ShapeDtypeStruct((EDGE_ROWS, HALF), jnp.float32),) * 2,
        tuple(base),
    )


def finish_body(totals, extra_refs, out_refs):
    low_ref, high_ref, weight_ref, proj_ref = extra_refs
    corner_ref, gram_ref = out_refs
    width = PANEL // D
    low = low_ref[...] + totals[0]
    high = high_ref[...] + totals[1]
    parts = [low[:, :width], low[:, width:], high[:, :width], high[:, width:]]
    mixed = []
    for t in range(D):
        total = None
        for u in range(D):
            term = parts[u] * weight_ref[:, u * D + t : u * D + t + 1]
            total = term if total is None else total + term
        mixed.append(total.astype(jnp.bfloat16))
    enlarged = jnp.concatenate(mixed, axis=1)
    projected = jnp.dot(enlarged, proj_ref[...], preferred_element_type=jnp.float32)
    corner_ref[...] = projected.astype(jnp.bfloat16)
    gram_ref[...] = lax.dot_general(
        projected,
        projected,
        (((0,), (0,)), ((), ())),
        precision=lax.Precision.HIGHEST,
        preferred_element_type=jnp.float32,
    )


def sort_kernel(corner_ref, out_ref):
    for y in range(NY):
        for z in range(NZ):
            for x in range(2):
                block = ((y * NZ + z) * 2 + x) * 128
                out_ref[y * 2 + x, :, z * 128 : (z + 1) * 128] = corner_ref[:, block : block + 128]


def sorted_columns(corner_rows):
    vmem = pl.BlockSpec(memory_space=pltpu.VMEM)
    return pl.pallas_call(
        sort_kernel,
        out_shape=jax.ShapeDtypeStruct((NY * 2, 128, NZ * 128), jnp.bfloat16),
        in_specs=[vmem],
        out_specs=vmem,
        compiler_params=pltpu.CompilerParams(vmem_limit_bytes=16 << 20),
        cost_estimate=pl.CostEstimate(flops=0, bytes_accessed=4 << 20, transcendentals=0),
    )(corner_rows)


def partial_kernel(pos_ref, corner_ref, *refs):
    piece_refs, out_refs = refs[:NZ], refs[NZ : NZ + 2 * NY]
    panel, edges, products = refs[NZ + 2 * NY :]
    for dz, piece_ref in enumerate(piece_refs):
        start = pl.multiple_of(lax.rem(pos_ref[1] + dz, NZ) * 128, 128)
        panel[pl.ds(start, 128), :] = piece_ref[...]
    held = panel[:, :PANEL]
    edges[...] = lax.dot_general(
        panel[:, PANEL:], held, (((0,), (0,)), ((), ())), preferred_element_type=jnp.float32
    )
    corner = corner_ref[...].reshape(NY * 2 * 128, NZ * 128)
    products[...] = jnp.dot(corner, held, preferred_element_type=jnp.float32).astype(jnp.bfloat16)
    for dy in range(NY):
        y = lax.rem(pos_ref[0] + dy, NY)
        hidden = products[pl.ds(pl.multiple_of(y * DEPTH, DEPTH), DEPTH), :]
        rows = edges[pl.ds(pl.multiple_of((y * NZ + pos_ref[1]) * 8, 8), 8), :]
        high = rows.astype(jnp.bfloat16).astype(jnp.float32)
        rows = jnp.concatenate([high, rows - high], axis=0).astype(jnp.bfloat16)
        for chain in range(2):
            out_ref = out_refs[chain * NY + dy]
            out_ref[:DEPTH] = hidden[:, chain * HALF : (chain + 1) * HALF]
            out_ref[DEPTH:] = rows[:, chain * HALF : (chain + 1) * HALF]


def partial_products(position, corner_part, pieces):
    vmem = pl.BlockSpec(memory_space=pltpu.VMEM)
    rows = DEPTH + 16
    return pl.pallas_call(
        partial_kernel,
        out_shape=(jax.ShapeDtypeStruct((rows, HALF), jnp.bfloat16),) * (2 * NY),
        in_specs=[pl.BlockSpec(memory_space=pltpu.SMEM)] + [vmem] * (1 + NZ),
        out_specs=(vmem,) * (2 * NY),
        scratch_shapes=[
            pltpu.VMEM((NZ * 128, PANEL + KEEP), jnp.bfloat16),
            pltpu.VMEM((KEEP, PANEL), jnp.float32),
            pltpu.VMEM((NY * DEPTH, PANEL), jnp.bfloat16),
        ],
        compiler_params=pltpu.CompilerParams(vmem_limit_bytes=24 << 20),
        cost_estimate=pl.CostEstimate(
            flops=2 * NY * rows * NZ * 128 * PANEL, bytes_accessed=4 << 20, transcendentals=0
        ),
    )(position, corner_part, *pieces)


def to_direction(block, shift, flip):
    directions = lax.axis_size("dir")
    route = [
        (k * 2 + x, ((k + shift) % directions) * 2 + (1 - x if flip else x))
        for k in range(directions)
        for x in range(2)
    ]
    return lax.ppermute(block, ("dir", "xh"), route)


def half_rows(block, which):
    return lax.dynamic_slice_in_dim(block, which * 4, 4, 0)


def on_device(corner_mat, edge_mat, edge_panel, vertex_weights, projector, edge_projector):
    corner_rows = corner_mat[0]
    panel_rows = edge_panel[0]
    xh = lax.axis_index("xh")
    position = jnp.stack([lax.axis_index("y"), lax.axis_index("z")]).astype(jnp.int32)
    edge_blocks = cut_edge(position, edge_mat[0])

    corner_part = lax.all_to_all(
        sorted_columns(corner_rows), ("y", "xh"), split_axis=0, concat_axis=0, tiled=True
    )
    up = down = jnp.concatenate([panel_rows, edge_projector[0]], axis=1)
    panel_part = {0: up}
    proj_next = fetched(projector[0], "dir", 1)
    for step in range(1, NZ // 2):
        up, down = fetched(up, "z", 1), fetched(down, "z", -1)
        panel_part[step], panel_part[NZ - step] = up, down
    panel_part[NZ // 2] = fetched(up, "z", 1)

    parts = partial_products(position, corner_part, [panel_part[dz] for dz in range(NZ)])
    blocks, edge_parts = [], []
    for chain in range(2):
        mine, *others = parts[chain * NY : (chain + 1) * NY]
        sums = mine.astype(jnp.float32)
        for dy in range(1, NY):
            sums = sums + fetched(others[dy - 1], "y", -dy).astype(jnp.float32)
        edge_parts.append(sums[DEPTH : DEPTH + 8] + sums[DEPTH + 8 :])
        partial = sums[:DEPTH].astype(jnp.bfloat16)
        same, other = to_direction(partial, -1, False), to_direction(partial, -1, True)
        blocks.append((same.astype(jnp.float32) + other.astype(jnp.float32)).astype(jnp.bfloat16))
    edge_part = jnp.concatenate(edge_parts, axis=1)
    left, right = blocks
    row_weights = jnp.tile(vertex_weights.reshape(D, D * D), (EDGE_ROWS // D, 1))

    cut = NY * DEPTH

    def all_y(dz):
        return [(dy, dz) for dy in range(NY)]

    def over_y(block):
        return [fetched(block, "y", dy) for dy in (1, 3, 2)]

    def pieces_y(arrays, dzs):
        return [(array, 0, [(dy, dz) for dz in dzs]) for array, dy in zip(arrays, (1, 3, 2))]

    def ring(up, down):
        return fetched(up, "z", 1), fetched(down, "z", -1)

    beside = over_y(right)
    up, down = ring(right, right)
    near = over_y(left)
    near, beside, up, down = tied(near, beside, up, down)

    row = jnp.concatenate([left, near[0], near[2], near[1]], axis=0)
    first = jnp.concatenate([up, down], axis=0)
    up, down = jnp.concatenate([row, up], axis=0), jnp.concatenate([row, down], axis=0)
    raws = raw_products(
        edge_blocks,
        [(row, 0, all_y(0))],
        [(right, 0, [(0, 0)]), (first, 0, [(0, 1), (0, 7)])] + pieces_y(beside, (0,)),
    )
    up, down = ring(up, down)
    batch = over_y(first)
    up, down, batch, raws = tied(up, down, batch, raws)

    second = jnp.concatenate([up[cut:], down[cut:]], axis=0)
    raws = raw_products(
        edge_blocks,
        [(up, 0, all_y(1)), (down, 0, all_y(7))],
        [(second, 0, [(0, 2), (0, 6)])] + pieces_y(batch, (1, 7)),
        raws,
    )
    up, down = ring(up, down)
    batch = over_y(second)
    up, down, batch, raws = tied(up, down, batch, raws)

    third = jnp.concatenate([up[cut:], down[cut:]], axis=0)
    raws = raw_products(
        edge_blocks,
        [(up, 0, all_y(2)), (down, 0, all_y(6))],
        [(third, 0, [(0, 3), (0, 5)])] + pieces_y(batch, (2, 6)),
        raws,
    )
    up, down = ring(up, down)
    batch = over_y(third)
    up, down, batch, raws = tied(up, down, batch, raws)

    fourth = up[cut:]
    raws = raw_products(
        edge_blocks,
        [(up, 0, all_y(3)), (down, 0, all_y(5))],
        [(fourth, 0, [(0, 4)])] + pieces_y(batch, (3, 5)),
        raws,
    )
    up, down, fourth, raws = tied(up, down, fourth, raws)
    top, bottom = ring(up[: cut // 2], down[cut // 2 : cut])
    batch = over_y(fourth)
    corner_here, partial_gram = run_products(
        edge_blocks,
        [
            Product([(top, 0, all_y(4)[:2]), (bottom, 0, all_y(4)[2:])]),
            Product(pieces_y(batch, (4,))),
        ],
        finish_body,
        (
            jax.ShapeDtypeStruct((EDGE_ROWS, KEEP), jnp.bfloat16),
            jax.ShapeDtypeStruct((KEEP, KEEP), jnp.float32),
        ),
        (raws[0], raws[1], row_weights, proj_next),
    )
    edge_part, corner_here = tied(edge_part, corner_here)
    edge_other = fetched(half_rows(edge_part, 1 - xh), "xh", 1)
    new_edge = (half_rows(edge_part, xh) + edge_other).astype(jnp.bfloat16)
    new_corner = fetched(corner_here, "dir", -1)
    partials = lax.all_to_all(
        partial_gram.reshape(NY * NZ, 8, KEEP), ("y", "z"), split_axis=0, concat_axis=0, tiled=True
    )
    gram_part = partials.sum(axis=0)
    gram = (
        to_direction(half_rows(gram_part, xh), 1, False)
        + to_direction(half_rows(gram_part, 1 - xh), 1, True)
    ) / (CHI * D)
    return (new_corner[None], gram[None], new_edge[None])


def solution(mesh):
    fine = Mesh(mesh.devices.reshape(4, NY, NZ, 2), ("dir", "y", "z", "xh"))
    rows = P("dir", ("y", "z", "xh"), None)
    in_specs = (rows, rows, rows, P(), P("dir", None, None), rows)
    return jax.shard_map(
        on_device, mesh=fine, in_specs=in_specs, out_specs=(rows, rows, rows), check_vma=False
    )
```

```python
import jax
import jax.numpy as jnp
from jax import lax
from jax.experimental import pallas as pl
from jax.experimental.pallas import tpu as pltpu
from jax.sharding import Mesh, PartitionSpec as P

CHI = 8192
D = 4
PANEL = 512
KEEP = 256
NY = 4
NZ = 8
HALF = PANEL // 2
GRANT = 14 << 20
CUT_GRANT = 16 << 20
EDGE_ROWS = CHI * D // 64
DEPTH = 256


def fetched(block, axis, distance):
    size = lax.axis_size(axis)
    return lax.ppermute(block, axis, [((i + distance) % size, i) for i in range(size)])


def tied(*values):
    return lax.optimization_barrier(values)


class Product:
    def __init__(self, pieces):
        self.pieces = pieces
        self.count = sum(len(table) for _, _, table in pieces)

    def run(self, edge_refs, piece_refs):
        total = None
        for (_, first, table), piece_ref in zip(self.pieces, piece_refs):
            piece = piece_ref[first : first + len(table) * DEPTH, :]
            left = jnp.concatenate([edge_refs[dz][dy] for dy, dz in table], axis=1)
            product = jnp.dot(left, piece, preferred_element_type=jnp.float32)
            total = product if total is None else total + product
        return total


def run_products(edge_blocks, products, body, out_shape, extra=()):
    arrays, needed = [], []
    for product in products:
        for array, _, table in product.pieces:
            if all(array is not other for other in arrays):
                arrays.append(array)
            needed += [dz for _, dz in table if dz not in needed]
    places = [
        [[array is other for other in arrays].index(True) for array, _, _ in product.pieces]
        for product in products
    ]
    outs = len(out_shape)

    def kernel(*refs):
        edge_refs, refs = dict(zip(needed, refs)), refs[len(needed) :]
        array_refs, refs = refs[: len(arrays)], refs[len(arrays) :]
        extra_refs, out_refs = refs[: len(extra)], refs[len(extra) :]
        totals = [
            product.run(edge_refs, [array_refs[i] for i in place])
            for product, place in zip(products, places)
        ]
        body(totals, extra_refs, out_refs)

    vmem = pl.BlockSpec(memory_space=pltpu.VMEM)
    count = sum(product.count for product in products)
    return pl.pallas_call(
        kernel,
        out_shape=out_shape,
        in_specs=[vmem] * (len(needed) + len(arrays) + len(extra)),
        out_specs=(vmem,) * outs,
        compiler_params=pltpu.CompilerParams(vmem_limit_bytes=GRANT),
        cost_estimate=pl.CostEstimate(
            flops=2 * EDGE_ROWS * HALF * count * DEPTH,
            bytes_accessed=2 * (EDGE_ROWS + HALF) * count * DEPTH,
            transcendentals=0,
        ),
    )(*[edge_blocks[dz] for dz in needed], *arrays, *extra)


def cut_kernel(pos_ref, edge_ref, *refs):
    out_refs, sems = refs[:NZ], refs[NZ]
    copies = []
    for dz in range(NZ):
        for dy in range(NY):
            block = lax.rem(pos_ref[0] + dy, NY) * NZ + lax.rem(pos_ref[1] + dz, NZ)
            copies.append(
                pltpu.make_async_copy(
                    edge_ref.at[:, pl.ds(pl.multiple_of(block * DEPTH, DEPTH), DEPTH)],
                    out_refs[dz].at[dy],
                    sems.at[dz, dy],
                )
            )
    for copy in copies:
        copy.start()
    for copy in copies:
        copy.wait()


def cut_edge(position, edge_rows):
    vmem = pl.BlockSpec(memory_space=pltpu.VMEM)
    return pl.pallas_call(
        cut_kernel,
        out_shape=(jax.ShapeDtypeStruct((NY, EDGE_ROWS, DEPTH), jnp.bfloat16),) * NZ,
        in_specs=[pl.BlockSpec(memory_space=pltpu.SMEM), pl.BlockSpec(memory_space=pl.ANY)],
        out_specs=(vmem,) * NZ,
        scratch_shapes=[pltpu.SemaphoreType.DMA((NZ, NY))],
        compiler_params=pltpu.CompilerParams(vmem_limit_bytes=CUT_GRANT),
        cost_estimate=pl.CostEstimate(flops=0, bytes_accessed=16 << 20, transcendentals=0),
    )(position, edge_rows)


def raw_body(totals, extra_refs, out_refs):
    for chain in range(2):
        total = totals[chain]
        if extra_refs:
            total = total + extra_refs[chain][...]
        out_refs[chain][...] = total
    if len(out_refs) > 2:
        middle = out_refs[2].shape[0]
        out_refs[2][...] = extra_refs[2][:middle]
        out_refs[3][...] = extra_refs[3][middle : 2 * middle]


def raw_products(edge_blocks, low_pieces, high_pieces, base=(), halved=()):
    return run_products(
        edge_blocks,
        [Product(low_pieces), Product(high_pieces)],
        raw_body,
        (jax.ShapeDtypeStruct((EDGE_ROWS, HALF), jnp.float32),) * 2
        + (jax.ShapeDtypeStruct((NY * DEPTH // 2, HALF), jnp.bfloat16),) * len(halved),
        tuple(base) + tuple(halved),
    )


def finish_body(totals, extra_refs, out_refs):
    low_ref, high_ref, weight_ref, proj_ref = extra_refs
    corner_ref, gram_ref = out_refs
    width = PANEL // D
    low = low_ref[...] + totals[0]
    high = high_ref[...] + totals[1]
    parts = [low[:, :width], low[:, width:], high[:, :width], high[:, width:]]
    mixed = []
    for t in range(D):
        total = None
        for u in range(D):
            term = parts[u] * weight_ref[:, u * D + t : u * D + t + 1]
            total = term if total is None else total + term
        mixed.append(total.astype(jnp.bfloat16))
    enlarged = jnp.concatenate(mixed, axis=1)
    projected = jnp.dot(enlarged, proj_ref[...], preferred_element_type=jnp.float32)
    corner_ref[...] = projected.astype(jnp.bfloat16)
    gram_ref[...] = lax.dot_general(
        projected,
        projected,
        (((0,), (0,)), ((), ())),
        precision=lax.Precision.HIGHEST,
        preferred_element_type=jnp.float32,
    )


def sort_kernel(corner_ref, out_ref):
    for y in range(NY):
        for z in range(NZ):
            for x in range(2):
                block = ((y * NZ + z) * 2 + x) * 128
                out_ref[y * 2 + x, :, z * 128 : (z + 1) * 128] = corner_ref[:, block : block + 128]


def sorted_columns(corner_rows):
    vmem = pl.BlockSpec(memory_space=pltpu.VMEM)
    return pl.pallas_call(
        sort_kernel,
        out_shape=jax.ShapeDtypeStruct((NY * 2, 128, NZ * 128), jnp.bfloat16),
        in_specs=[vmem],
        out_specs=vmem,
        compiler_params=pltpu.CompilerParams(vmem_limit_bytes=16 << 20),
        cost_estimate=pl.CostEstimate(flops=0, bytes_accessed=4 << 20, transcendentals=0),
    )(corner_rows)


def partial_kernel(pos_ref, corner_ref, *refs):
    piece_refs, out_refs = refs[:NZ], refs[NZ : NZ + 2 * NY]
    panel, edges, products = refs[NZ + 2 * NY :]
    for dz, piece_ref in enumerate(piece_refs):
        start = pl.multiple_of(lax.rem(pos_ref[1] + dz, NZ) * 128, 128)
        panel[pl.ds(start, 128), :] = piece_ref[...]
    held = panel[:, :PANEL]
    edges[...] = lax.dot_general(
        panel[:, PANEL:], held, (((0,), (0,)), ((), ())), preferred_element_type=jnp.float32
    )
    corner = corner_ref[...].reshape(NY * 2 * 128, NZ * 128)
    products[...] = jnp.dot(corner, held, preferred_element_type=jnp.float32).astype(jnp.bfloat16)
    for dy in range(NY):
        y = lax.rem(pos_ref[0] + dy, NY)
        hidden = products[pl.ds(pl.multiple_of(y * DEPTH, DEPTH), DEPTH), :]
        rows = edges[pl.ds(pl.multiple_of((y * NZ + pos_ref[1]) * 8, 8), 8), :]
        high = rows.astype(jnp.bfloat16).astype(jnp.float32)
        rows = jnp.concatenate([high, rows - high], axis=0).astype(jnp.bfloat16)
        for chain in range(2):
            out_ref = out_refs[chain * NY + dy]
            out_ref[:DEPTH] = hidden[:, chain * HALF : (chain + 1) * HALF]
            out_ref[DEPTH:] = rows[:, chain * HALF : (chain + 1) * HALF]


def partial_products(position, corner_part, pieces):
    vmem = pl.BlockSpec(memory_space=pltpu.VMEM)
    rows = DEPTH + 16
    return pl.pallas_call(
        partial_kernel,
        out_shape=(jax.ShapeDtypeStruct((rows, HALF), jnp.bfloat16),) * (2 * NY),
        in_specs=[pl.BlockSpec(memory_space=pltpu.SMEM)] + [vmem] * (1 + NZ),
        out_specs=(vmem,) * (2 * NY),
        scratch_shapes=[
            pltpu.VMEM((NZ * 128, PANEL + KEEP), jnp.bfloat16),
            pltpu.VMEM((KEEP, PANEL), jnp.float32),
            pltpu.VMEM((NY * DEPTH, PANEL), jnp.bfloat16),
        ],
        compiler_params=pltpu.CompilerParams(vmem_limit_bytes=24 << 20),
        cost_estimate=pl.CostEstimate(
            flops=2 * NY * rows * NZ * 128 * PANEL, bytes_accessed=4 << 20, transcendentals=0
        ),
    )(position, corner_part, *pieces)


def to_direction(block, shift, flip):
    directions = lax.axis_size("dir")
    route = [
        (k * 2 + x, ((k + shift) % directions) * 2 + (1 - x if flip else x))
        for k in range(directions)
        for x in range(2)
    ]
    return lax.ppermute(block, ("dir", "xh"), route)


def half_rows(block, which):
    return lax.dynamic_slice_in_dim(block, which * 4, 4, 0)


def on_device(corner_mat, edge_mat, edge_panel, vertex_weights, projector, edge_projector):
    corner_rows = corner_mat[0]
    panel_rows = edge_panel[0]
    xh = lax.axis_index("xh")
    position = jnp.stack([lax.axis_index("y"), lax.axis_index("z")]).astype(jnp.int32)
    edge_blocks = cut_edge(position, edge_mat[0])

    corner_part = lax.all_to_all(
        sorted_columns(corner_rows), ("y", "xh"), split_axis=0, concat_axis=0, tiled=True
    )
    up = down = jnp.concatenate([panel_rows, edge_projector[0]], axis=1)
    panel_part = {0: up}
    proj_next = fetched(projector[0], "dir", 1)
    for step in range(1, NZ // 2):
        up, down = fetched(up, "z", 1), fetched(down, "z", -1)
        panel_part[step], panel_part[NZ - step] = up, down
    panel_part[NZ // 2] = fetched(up, "z", 1)

    parts = partial_products(position, corner_part, [panel_part[dz] for dz in range(NZ)])
    blocks, edge_parts = [], []
    for chain in range(2):
        mine, *others = parts[chain * NY : (chain + 1) * NY]
        sums = mine.astype(jnp.float32)
        for dy in range(1, NY):
            sums = sums + fetched(others[dy - 1], "y", -dy).astype(jnp.float32)
        edge_parts.append(sums[DEPTH : DEPTH + 8] + sums[DEPTH + 8 :])
        partial = sums[:DEPTH].astype(jnp.bfloat16)
        same, other = to_direction(partial, -1, False), to_direction(partial, -1, True)
        blocks.append((same.astype(jnp.float32) + other.astype(jnp.float32)).astype(jnp.bfloat16))
    edge_part = jnp.concatenate(edge_parts, axis=1)
    left, right = blocks
    row_weights = jnp.tile(vertex_weights.reshape(D, D * D), (EDGE_ROWS // D, 1))

    cut = NY * DEPTH

    def all_y(dz):
        return [(dy, dz) for dy in range(NY)]

    def over_y(block):
        return [fetched(block, "y", dy) for dy in (1, 3, 2)]

    def pieces_y(arrays, dzs):
        return [(array, 0, [(dy, dz) for dz in dzs]) for array, dy in zip(arrays, (1, 3, 2))]

    def ring(up, down):
        return fetched(up, "z", 1), fetched(down, "z", -1)

    beside = over_y(right)
    up, down = ring(right, right)
    near = over_y(left)
    near, beside, up, down = tied(near, beside, up, down)

    row = jnp.concatenate([left, near[0], near[2], near[1]], axis=0)
    first = jnp.concatenate([up, down], axis=0)
    up, down = jnp.concatenate([row, up], axis=0), jnp.concatenate([row, down], axis=0)
    raws = raw_products(
        edge_blocks,
        [(row, 0, all_y(0))],
        [(right, 0, [(0, 0)]), (first, 0, [(0, 1), (0, 7)])] + pieces_y(beside, (0,)),
    )
    up, down = ring(up, down)
    batch = over_y(first)
    up, down, batch, raws = tied(up, down, batch, raws)

    second = jnp.concatenate([up[cut:], down[cut:]], axis=0)
    raws = raw_products(
        edge_blocks,
        [(up, 0, all_y(1)), (down, 0, all_y(7))],
        [(second, 0, [(0, 2), (0, 6)])] + pieces_y(batch, (1, 7)),
        raws,
    )
    up, down = ring(up, down)
    batch = over_y(second)
    up, down, batch, raws = tied(up, down, batch, raws)

    third = jnp.concatenate([up[cut:], down[cut:]], axis=0)
    raws = raw_products(
        edge_blocks,
        [(up, 0, all_y(2)), (down, 0, all_y(6))],
        [(third, 0, [(0, 3), (0, 5)])] + pieces_y(batch, (2, 6)),
        raws,
    )
    up, down = ring(up, down)
    batch = over_y(third)
    up, down, batch, raws = tied(up, down, batch, raws)

    fourth = up[cut:]
    *raws, up, down = raw_products(
        edge_blocks,
        [(up, 0, all_y(3)), (down, 0, all_y(5))],
        [(fourth, 0, [(0, 4)])] + pieces_y(batch, (3, 5)),
        raws,
        (up, down),
    )
    up, down, fourth, raws = tied(up, down, fourth, raws)
    top, bottom = ring(up, down)
    batch = over_y(fourth)
    corner_here, partial_gram = run_products(
        edge_blocks,
        [
            Product([(top, 0, all_y(4)[:2]), (bottom, 0, all_y(4)[2:])]),
            Product(pieces_y(batch, (4,))),
        ],
        finish_body,
        (
            jax.ShapeDtypeStruct((EDGE_ROWS, KEEP), jnp.bfloat16),
            jax.ShapeDtypeStruct((KEEP, KEEP), jnp.float32),
        ),
        (raws[0], raws[1], row_weights, proj_next),
    )
    edge_part, corner_here = tied(edge_part, corner_here)
    edge_other = fetched(half_rows(edge_part, 1 - xh), "xh", 1)
    new_edge = (half_rows(edge_part, xh) + edge_other).astype(jnp.bfloat16)
    new_corner = fetched(corner_here, "dir", -1)
    partials = lax.all_to_all(
        partial_gram.reshape(NY * NZ * 2, 4, KEEP),
        ("y", "z", "xh"),
        split_axis=0,
        concat_axis=0,
        tiled=True,
    )
    gram = fetched(partials.sum(axis=0) / (CHI * D), "dir", -1)
    return (new_corner[None], gram[None], new_edge[None])


def solution(mesh):
    fine = Mesh(mesh.devices.reshape(4, NY, NZ, 2), ("dir", "y", "z", "xh"))
    rows = P("dir", ("y", "z", "xh"), None)
    in_specs = (rows, rows, rows, P(), P("dir", None, None), rows)
    return jax.shard_map(
        on_device, mesh=fine, in_specs=in_specs, out_specs=(rows, rows, rows), check_vma=False
    )
```
